32 devices in a mesh: freq: 2 (over x), row: 16 (over z, y, core).
Axes of the slice: x: 2, y: 2, z: 4, core: 2. Of those that a mesh axis runs over, the one named last changes fastest.
Arguments:
- p_panel: float32 [2, 256, 256], P(None, ('freq', 'row')), parts along dimension 1, may hold values from -0.375 to 0.375
- eps_coef: float32 [4, 201, 201], P('freq'), parts along dimension 0, may hold values from -3 to 3
- inv_coef: float32 [4, 201, 201], P('freq'), parts along dimension 0, may hold values from -3 to 3
- wave: float32 [8], P('freq'), parts along dimension 0, may hold values from 0.02 to 0.06
- harmonics: int32 [2, 2048], replicated, may hold values from -50 to 50, as said below
- panel: int32 [256], replicated, may hold values from 0 to 4095, as said below
- row_target: int32 [128], replicated, may hold values from 0 to 127, as said below
Outputs:
- omega: float32 [2, 256, 4096], P(None, ('freq', 'row')), parts along dimension 1
The draws below stay inside these ranges and needn't reach their ends.
There are 2 independent parts, one for each index of `freq`. The reference program is written for one: setup_inputs(seed, part) draws one part's arguments, and reference() takes and returns one part's arrays. A program takes and returns all parts, laid end to end along the dimension named above; an argument that names none is the same for every part. Nothing has to cross between parts.
Inputs may be any that keep to these rules, and one draw needn't show every extreme that they name: `harmonics`: all pairs (m, n) are distinct. `panel`: 256 distinct row indices of Q. row_target[s] = 8 rho(s mod 16) + tau(s // 16) for a permutation rho of 0 .. 15 and a permutation tau of 0 .. 7, both drawn from the seed; each window row appears once.
All inputs are finite; a program needn't handle non-finite values.
Results may differ from the reference program's by a relative error of at most 0.0003.
Values sent between devices are 32-bit elements; how exact they have to be, the bound alone decides.
A program may use at most 128 MiB of HBM per device.

```python
import jax
import jax.numpy as jnp
from jax import lax

MAXORD = 50
HARM_DEV = 128
PANEL = 256
ROW_DEV = 8
HARM = 2048
ORDER = 4096
ROWS = 128
N_ROW = 16


def draw_harmonics(key, part):
    extent = 2 * MAXORD + 1
    chosen_ids = jax.random.permutation(key, extent * extent)[:HARM]
    return jnp.stack([chosen_ids // extent - MAXORD, chosen_ids % extent - MAXORD]).astype(jnp.int32)


def draw_panel(key, part):
    return jax.random.permutation(jax.random.fold_in(key, 7), ORDER)[:PANEL].astype(jnp.int32)


def draw_row_target(key, part):
    source_order = jax.random.permutation(jax.random.fold_in(key, 11), N_ROW).astype(jnp.int32)
    local_order = jax.random.permutation(jax.random.fold_in(key, 13), ROW_DEV).astype(jnp.int32)
    positions = jnp.arange(ROWS, dtype=jnp.int32)
    return (jnp.take(source_order, positions % N_ROW) * ROW_DEV + jnp.take(local_order, positions // N_ROW)).astype(jnp.int32)


def block_scale(own_key, shape, cuts, low, top_value):
    level, own = 1.0, jax.random.fold_in(own_key, 6)
    for dim, shards_of in cuts:
        draws = jnp.exp(jax.random.uniform(jax.random.fold_in(own, dim), (shards_of,), jnp.float32, low / len(cuts), top_value / len(cuts)))
        level = level * jnp.repeat(draws, shape[dim] // shards_of).reshape([-1 if axis == dim else 1 for axis in range(len(shape))])
    return level


def gaussian(own_key, shape, width, most, cuts=(), kind=jnp.bfloat16):
    values = jax.random.normal(own_key, shape, jnp.float32) * width
    if len(cuts) > 0:
        values = block_scale(own_key, shape, cuts, -0.22, 0.18) * values
    return jnp.clip(values, min=-most, max=most).astype(kind)


def setup_inputs(seed: int = 0, part: int = 0) -> dict:
    arg_keys = jax.random.split(jax.random.key(seed), 8)
    own_keys = jax.random.split(jax.random.fold_in(arg_keys[7], part), 8)
    return {
        "p_panel": gaussian(own_keys[0], (2, ROWS, PANEL), PANEL ** -0.5, 0.375, ((1, 16),), jnp.float32),
        "eps_coef": gaussian(own_keys[1], (2, 4 * MAXORD + 1, 4 * MAXORD + 1), 0.5, 3.0, (), jnp.float32),
        "inv_coef": gaussian(own_keys[2], (2, 4 * MAXORD + 1, 4 * MAXORD + 1), 0.5, 3.0, (), jnp.float32),
        "wave": jnp.clip(jax.random.uniform(own_keys[3], (4,), jnp.float32, 0.02, 0.06), 0.02, 0.06),
        "harmonics": draw_harmonics(jax.random.fold_in(arg_keys[7], 71), part),
        "panel": draw_panel(jax.random.fold_in(arg_keys[7], 71), part),
        "row_target": draw_row_target(jax.random.fold_in(arg_keys[7], 71), part),
    }


def build_panel(harmonics, panel, eps_coef, inv_coef, wave, first_col, col_count):
    harm_total = harmonics.shape[1]
    row_block = panel // harm_total
    row_harm = panel % harm_total
    m_row = jnp.take(harmonics[0], row_harm)
    n_row = jnp.take(harmonics[1], row_harm)
    col_harm = first_col + jnp.arange(col_count, dtype=jnp.int32)
    m_col = lax.dynamic_slice_in_dim(harmonics[0], first_col, col_count)
    n_col = lax.dynamic_slice_in_dim(harmonics[1], first_col, col_count)
    centre = (eps_coef.shape[1] - 1) // 2
    offset_m = m_row[:, None] - m_col[None, :] + centre
    offset_n = n_row[:, None] - n_col[None, :] + centre
    table_index = offset_m * eps_coef.shape[2] + offset_n
    eps_real = jnp.take(eps_coef[0].reshape(-1), table_index)
    eps_imag = jnp.take(eps_coef[1].reshape(-1), table_index)
    inv_real = jnp.take(inv_coef[0].reshape(-1), table_index)
    inv_imag = jnp.take(inv_coef[1].reshape(-1), table_index)
    wave_x = (wave[0] + m_row.astype(jnp.float32) * wave[2])[:, None]
    wave_y = (wave[1] + n_row.astype(jnp.float32) * wave[3])[:, None]
    on_diag = (row_harm[:, None] == col_harm[None, :]).astype(jnp.float32)
    top_half = (row_block == 0)[:, None]
    zeros_like = jnp.zeros_like(eps_real)
    first_real = jnp.where(top_half, wave_x * wave_y * on_diag, wave_y * wave_y * on_diag - eps_real)
    first_imag = jnp.where(top_half, zeros_like, -eps_imag)
    second_real = jnp.where(top_half, inv_real - wave_x * wave_x * on_diag, -wave_x * wave_y * on_diag)
    second_imag = jnp.where(top_half, inv_imag, zeros_like)
    return jnp.stack([jnp.concatenate([first_real, second_real], 1), jnp.concatenate([first_imag, second_imag], 1)])


def matmul(first_mat, second_mat):
    return jnp.dot(first_mat, second_mat, precision=lax.Precision.HIGHEST, preferred_element_type=jnp.float32)


def complex_product(first_mat, second_mat):
    real_part = matmul(first_mat[0], second_mat[0]) - matmul(first_mat[1], second_mat[1])
    imag_part = matmul(first_mat[0], second_mat[1]) + matmul(first_mat[1], second_mat[0])
    return jnp.stack([real_part, imag_part])


def reference(p_panel, eps_coef, inv_coef, wave, harmonics, panel, row_target):
    selected = jnp.take(p_panel, row_target, axis=1)

    def per_block(block_id):
        q_part = build_panel(harmonics, panel, eps_coef, inv_coef, wave, block_id * HARM_DEV, HARM_DEV)
        return complex_product(selected, q_part)

    results = lax.map(per_block, jnp.arange(N_ROW, dtype=jnp.int32))
    return jnp.transpose(results, (1, 2, 0, 3)).reshape(2, selected.shape[1], N_ROW * 2 * HARM_DEV)
```

```python
import functools

import jax
import jax.numpy as jnp
from jax import lax
from jax.experimental import pallas as pl
from jax.experimental.pallas import tpu as pltpu
from jax.sharding import PartitionSpec as P

LANES = 128
SUB = 8
UNROLL = 8


def round_up(value, step):
    return -(-value // step) * step


def build_q(me, extent, dims, eps_ref, inv_ref, wave_ref, harm_s, harm_v, panel_s, tab, part, q_ref):
    harm_total, cols, depth = dims
    half = (extent - 1) // 4
    window = round_up(2 * half + 1, SUB)
    rows_tab = round_up(extent + window - 2 * half - 1, SUB)
    i32 = jnp.int32
    lane = lax.broadcasted_iota(i32, (SUB, LANES), 1)
    sub = lax.broadcasted_iota(i32, (SUB, LANES), 0)
    first = pl.multiple_of(me * cols, cols)
    orders = harm_v[:, pl.ds(first, cols)]
    m_col = jnp.broadcast_to(orders[0:1, :], (SUB, cols))
    n_col = jnp.broadcast_to(orders[1:2, :], (SUB, cols))
    row_pick = half - m_col - sub
    col_base = 2 * half - n_col
    own = jnp.where(sub == 0, first + lane, -1)

    def block(step, carry):
        for u in range(UNROLL):
            k = step * UNROLL + u
            row = panel_s[k]
            bottom = row >= harm_total
            h = jnp.where(bottom, row - harm_total, row)
            m = harm_s[0, h]
            n = harm_s[1, h]
            start = n + half
            base = jnp.where(bottom, 4 * rows_tab, 0) + m + half
            index = (n + col_base) & (LANES - 1)
            low = lane >= start
            values = []
            for c in range(2):
                acc = jnp.zeros((SUB, LANES), jnp.float32)
                for i in range(window // SUB):
                    at = base + (2 * c * rows_tab + i * SUB)
                    left = tab[pl.ds(at, SUB), :]
                    right = tab[pl.ds(at + rows_tab, SUB), :]
                    both = jnp.where(low, left, right)
                    got = jnp.take_along_axis(both, index, axis=1, mode="promise_in_bounds")
                    acc = jnp.where(row_pick == i * SUB, got, acc)
                values.append(acc)
            wave_x = wave_ref[0] + m.astype(jnp.float32) * wave_ref[2]
            wave_y = wave_ref[1] + n.astype(jnp.float32) * wave_ref[3]
            sign0 = jnp.where(bottom, -1.0, 0.0)
            sign1 = jnp.where(bottom, 0.0, 1.0)
            diag0 = jnp.where(bottom, wave_y * wave_y, wave_x * wave_y)
            diag1 = jnp.where(bottom, -wave_x * wave_y, -wave_x * wave_x)
            on = own == h
            here = pl.ds(u * SUB, SUB)
            part[0, here, :] = values[0] * sign0 + jnp.where(on, diag0, 0.0)
            part[1, here, :] = values[0] * sign1 + jnp.where(on, diag1, 0.0)
            part[2, here, :] = values[1] * sign0
            part[3, here, :] = values[1] * sign1
        rows = pl.ds(pl.multiple_of(step * UNROLL, UNROLL), UNROLL)
        for c in range(4):
            total = part[c, pl.ds(0, UNROLL, stride=SUB), :]
            for s in range(1, SUB):
                total = total + part[c, pl.ds(s, UNROLL, stride=SUB), :]
            q_ref[rows, c * LANES : (c + 1) * LANES] = total
        return carry

    lax.fori_loop(0, depth // UNROLL, block, 0)


def fill_tables(extent, rows_tab, eps_ref, inv_ref, tab):
    for t, ref in enumerate((inv_ref, eps_ref)):
        for c in range(2):
            at = (4 * t + 2 * c) * rows_tab
            tab[at : at + extent, :] = ref[c, :, 0:LANES]
            tab[at + rows_tab : at + rows_tab + extent, 0 : extent - LANES] = ref[c, :, LANES:extent]


def kernel(
    n, extent, dims, p_ref, eps_ref, inv_ref, wave_ref, harm_s, harm_v, panel_s, target_ref, out_ref,
    tab, part, q_ref, p_all, prod, send_p, recv_p, send_o, recv_o, own_sem,
):
    harm_total, cols, depth = dims
    me = lax.axis_index("row")
    half = (extent - 1) // 4
    window = round_up(2 * half + 1, SUB)
    rows_tab = round_up(extent + window - 2 * half - 1, SUB)
    here = p_ref.shape[1]
    rows = n * here
    wide = 2 * cols

    barrier = pltpu.get_barrier_semaphore()

    def peer(d):
        return lax.rem(me + d, n)

    def greet(d, carry):
        pl.semaphore_signal(barrier, inc=1, device_id={"row": peer(d)}, device_id_type=pl.DeviceIdType.MESH)
        return carry

    lax.fori_loop(1, n, greet, 0)
    fill_tables(extent, rows_tab, eps_ref, inv_ref, tab)
    pl.semaphore_wait(barrier, n - 1)

    def p_copy(d):
        return pltpu.make_async_remote_copy(
            src_ref=p_ref,
            dst_ref=p_all.at[me],
            send_sem=send_p.at[d],
            recv_sem=recv_p.at[d],
            device_id={"row": peer(d)},
            device_id_type=pl.DeviceIdType.MESH,
        )

    def start_p(d, carry):
        p_copy(d).start()
        return carry

    lax.fori_loop(1, n, start_p, 0)
    p_all[me] = p_ref[...]

    build_q(me, extent, dims, eps_ref, inv_ref, wave_ref, harm_s, harm_v, panel_s, tab, part, q_ref)

    def wait_p(d, carry):
        p_copy(d).wait()
        return carry

    lax.fori_loop(1, n, wait_p, 0)

    pick = (lax.broadcasted_iota(jnp.int32, (rows, rows), 0) == target_ref[...]).astype(jnp.float32)
    q = q_ref[...]

    def permuted(c):
        return lax.dot_general(
            pick, p_all[:, c].reshape(rows, depth), (((0,), (0,)), ((), ())),
            precision=lax.Precision.HIGHEST, preferred_element_type=jnp.float32,
        )

    def times(left):
        return jnp.dot(left, q, precision=lax.Precision.HIGHEST, preferred_element_type=jnp.float32)

    by_real = times(permuted(0))
    by_imag = times(permuted(1))
    prod[:, 0] = (by_real[:, :wide] - by_imag[:, wide:]).reshape(n, here, wide)
    prod[:, 1] = (by_real[:, wide:] + by_imag[:, :wide]).reshape(n, here, wide)

    mine = pl.ds(pl.multiple_of(me * wide, wide), wide)

    def o_copy(d):
        return pltpu.make_async_remote_copy(
            src_ref=prod.at[peer(d)],
            dst_ref=out_ref.at[:, :, mine],
            send_sem=send_o.at[d],
            recv_sem=recv_o.at[d],
            device_id={"row": peer(d)},
            device_id_type=pl.DeviceIdType.MESH,
        )

    def start_o(d, carry):
        o_copy(d).start()
        return carry

    lax.fori_loop(1, n, start_o, 0)
    keep = pltpu.make_async_copy(prod.at[me], out_ref.at[:, :, mine], own_sem)
    keep.start()
    keep.wait()

    def wait_o(d, carry):
        o_copy(d).wait()
        return carry

    lax.fori_loop(1, n, wait_o, 0)


def on_device(n, p_panel, eps_coef, inv_coef, wave, harmonics, panel, row_target):
    extent = eps_coef.shape[1]
    harm_total = harmonics.shape[1]
    cols = harm_total // n
    depth = panel.shape[0]
    here = p_panel.shape[1]
    half = (extent - 1) // 4
    window = round_up(2 * half + 1, SUB)
    rows_tab = round_up(extent + window - 2 * half - 1, SUB)
    vmem = pl.BlockSpec(memory_space=pltpu.VMEM)
    smem = pl.BlockSpec(memory_space=pltpu.SMEM)
    f32 = jnp.float32
    return pl.pallas_call(
        functools.partial(kernel, n, extent, (harm_total, cols, depth)),
        out_shape=jax.ShapeDtypeStruct((2, here, n * 2 * cols), f32),
        in_specs=[vmem, vmem, vmem, smem, smem, vmem, smem, vmem],
        out_specs=vmem,
        scratch_shapes=[
            pltpu.VMEM((8 * rows_tab, LANES), f32),
            pltpu.VMEM((4, UNROLL * SUB, LANES), f32),
            pltpu.VMEM((depth, 4 * cols), f32),
            pltpu.VMEM((n, 2, here, depth), f32),
            pltpu.VMEM((n, 2, here, 2 * cols), f32),
            pltpu.SemaphoreType.DMA((n,)),
            pltpu.SemaphoreType.DMA((n,)),
            pltpu.SemaphoreType.DMA((n,)),
            pltpu.SemaphoreType.DMA((n,)),
            pltpu.SemaphoreType.DMA,
        ],
        compiler_params=pltpu.CompilerParams(
            collective_id=0, has_side_effects=True, vmem_limit_bytes=40 * 1024 * 1024
        ),
    )(p_panel, eps_coef, inv_coef, wave, harmonics, harmonics, panel, row_target.reshape(1, -1))


def solution(mesh):
    in_specs = (
        P(None, ("freq", "row"), None),
        P("freq", None, None),
        P("freq", None, None),
        P("freq"),
        P(),
        P(),
        P(),
    )
    return jax.shard_map(
        functools.partial(on_device, mesh.shape["row"]),
        mesh=mesh,
        in_specs=in_specs,
        out_specs=P(None, ("freq", "row"), None),
        check_vma=False,
    )
```

```python
import functools

import jax
import jax.numpy as jnp
from jax import lax
from jax.experimental import pallas as pl
from jax.experimental.pallas import tpu as pltpu
from jax.sharding import PartitionSpec as P

LANES = 128
SUB = 8
UNROLL = 16


def round_up(value, step):
    return -(-value // step) * step


def build_q(me, extent, dims, span, wave_ref, harm_s, harm_v, panel_s, tab, part, q_ref):
    harm_total, cols, _ = dims
    half = (extent - 1) // 4
    window = round_up(2 * half + 1, SUB)
    rows_tab = round_up(extent + window - 2 * half - 1, SUB)
    i32 = jnp.int32
    lane = lax.broadcasted_iota(i32, (SUB, LANES), 1)
    sub = lax.broadcasted_iota(i32, (SUB, LANES), 0)
    first = pl.multiple_of(me * cols, cols)
    orders = harm_v[:, pl.ds(first, cols)]
    m_col = jnp.broadcast_to(orders[0:1, :], (SUB, cols))
    n_col = jnp.broadcast_to(orders[1:2, :], (SUB, cols))
    row_pick = half - m_col - sub
    col_base = 2 * half - n_col
    own = jnp.where(sub == 0, first + lane, -1)

    def block(step, carry):
        for u in range(UNROLL):
            k = step * UNROLL + u
            row = panel_s[k]
            bottom = row >= harm_total
            h = jnp.where(bottom, row - harm_total, row)
            m = harm_s[0, h]
            n = harm_s[1, h]
            start = n + half
            base = jnp.where(bottom, 4 * rows_tab, 0) + m + half
            index = (n + col_base) & (LANES - 1)
            low = lane >= start
            values = []
            for c in range(2):
                acc = jnp.zeros((SUB, LANES), jnp.float32)
                for i in range(window // SUB):
                    at = base + (2 * c * rows_tab + i * SUB)
                    left = tab[pl.ds(at, SUB), :]
                    right = tab[pl.ds(at + rows_tab, SUB), :]
                    both = jnp.where(low, left, right)
                    got = jnp.take_along_axis(both, index, axis=1, mode="promise_in_bounds")
                    acc = jnp.where(row_pick == i * SUB, got, acc)
                values.append(acc)
            wave_x = wave_ref[0] + m.astype(jnp.float32) * wave_ref[2]
            wave_y = wave_ref[1] + n.astype(jnp.float32) * wave_ref[3]
            sign0 = jnp.where(bottom, -1.0, 0.0)
            sign1 = jnp.where(bottom, 0.0, 1.0)
            diag0 = jnp.where(bottom, wave_y * wave_y, wave_x * wave_y)
            diag1 = jnp.where(bottom, -wave_x * wave_y, -wave_x * wave_x)
            on = own == h
            here = pl.ds(u * SUB, SUB)
            part[0, here, :] = values[0] * sign0 + jnp.where(on, diag0, 0.0)
            part[1, here, :] = values[0] * sign1 + jnp.where(on, diag1, 0.0)
            part[2, here, :] = values[1] * sign0
            part[3, here, :] = values[1] * sign1
        rows = pl.ds(pl.multiple_of(step * UNROLL, UNROLL), UNROLL)
        for c in range(4):
            total = part[c, pl.ds(0, UNROLL, stride=SUB), :]
            for s in range(1, SUB):
                total = total + part[c, pl.ds(s, UNROLL, stride=SUB), :]
            q_ref[rows, c * LANES : (c + 1) * LANES] = total
        return carry

    lax.fori_loop(span[0], span[1], block, 0)


def fill_tables(extent, rows_tab, eps_ref, inv_ref, tab):
    for t, ref in enumerate((inv_ref, eps_ref)):
        for c in range(2):
            at = (4 * t + 2 * c) * rows_tab
            tab[at : at + extent, :] = ref[c, :, 0:LANES]
            tab[at + rows_tab : at + rows_tab + extent, 0 : extent - LANES] = ref[c, :, LANES:extent]


def kernel(
    n, extent, dims, p_ref, eps_ref, inv_ref, wave_ref, harm_s, harm_v, panel_s, target_ref, out_ref,
    tab, part, q_ref, p_all, prod, send_p, recv_p, send_o, recv_o, own_sem,
):
    harm_total, cols, depth = dims
    me = lax.axis_index("row")
    half = (extent - 1) // 4
    window = round_up(2 * half + 1, SUB)
    rows_tab = round_up(extent + window - 2 * half - 1, SUB)
    here = p_ref.shape[1]
    rows = n * here
    wide = 2 * cols

    barrier = pltpu.get_barrier_semaphore()

    def peer(d):
        return lax.rem(me + d, n)

    def greet(d, carry):
        pl.semaphore_signal(barrier, inc=1, device_id={"row": peer(d)}, device_id_type=pl.DeviceIdType.MESH)
        return carry

    lax.fori_loop(1, n, greet, 0)
    p_all[me] = p_ref[...]
    fill_tables(extent, rows_tab, eps_ref, inv_ref, tab)

    def build(begin, end):
        build_q(me, extent, dims, (begin, end), wave_ref, harm_s, harm_v, panel_s, tab, part, q_ref)

    steps = depth // UNROLL
    early = steps // 4
    build(0, early)
    pl.semaphore_wait(barrier, n - 1)

    def p_copy(d):
        return pltpu.make_async_remote_copy(
            src_ref=p_ref,
            dst_ref=p_all.at[me],
            send_sem=send_p.at[d],
            recv_sem=recv_p.at[d],
            device_id={"row": peer(d)},
            device_id_type=pl.DeviceIdType.MESH,
        )

    def start_p(d, carry):
        p_copy(d).start()
        return carry

    lax.fori_loop(1, n, start_p, 0)
    build(early, steps)

    def wait_p(d, carry):
        p_copy(d).wait()
        return carry

    lax.fori_loop(1, n, wait_p, 0)

    pick = (lax.broadcasted_iota(jnp.int32, (rows, rows), 0) == target_ref[...]).astype(jnp.float32)
    q = q_ref[...]

    def permuted(c):
        return lax.dot_general(
            pick, p_all[:, c].reshape(rows, depth), (((0,), (0,)), ((), ())),
            precision=lax.Precision.HIGHEST, preferred_element_type=jnp.float32,
        )

    def times(left):
        return jnp.dot(left, q, precision=lax.Precision.HIGHEST, preferred_element_type=jnp.float32)

    by_real = times(permuted(0))
    by_imag = times(permuted(1))
    prod[:, 0] = (by_real[:, :wide] - by_imag[:, wide:]).reshape(n, here, wide)
    prod[:, 1] = (by_real[:, wide:] + by_imag[:, :wide]).reshape(n, here, wide)

    mine = pl.ds(pl.multiple_of(me * wide, wide), wide)

    def o_copy(d):
        return pltpu.make_async_remote_copy(
            src_ref=prod.at[peer(d)],
            dst_ref=out_ref.at[:, :, mine],
            send_sem=send_o.at[d],
            recv_sem=recv_o.at[d],
            device_id={"row": peer(d)},
            device_id_type=pl.DeviceIdType.MESH,
        )

    def start_o(d, carry):
        o_copy(d).start()
        return carry

    lax.fori_loop(1, n, start_o, 0)
    keep = pltpu.make_async_copy(prod.at[me], out_ref.at[:, :, mine], own_sem)
    keep.start()
    keep.wait()

    def wait_o(d, carry):
        o_copy(d).wait()
        return carry

    lax.fori_loop(1, n, wait_o, 0)


def on_device(n, p_panel, eps_coef, inv_coef, wave, harmonics, panel, row_target):
    extent = eps_coef.shape[1]
    harm_total = harmonics.shape[1]
    cols = harm_total // n
    depth = panel.shape[0]
    here = p_panel.shape[1]
    half = (extent - 1) // 4
    window = round_up(2 * half + 1, SUB)
    rows_tab = round_up(extent + window - 2 * half - 1, SUB)
    vmem = pl.BlockSpec(memory_space=pltpu.VMEM)
    smem = pl.BlockSpec(memory_space=pltpu.SMEM)
    f32 = jnp.float32
    return pl.pallas_call(
        functools.partial(kernel, n, extent, (harm_total, cols, depth)),
        out_shape=jax.ShapeDtypeStruct((2, here, n * 2 * cols), f32),
        in_specs=[vmem, vmem, vmem, smem, smem, vmem, smem, vmem],
        out_specs=vmem,
        scratch_shapes=[
            pltpu.VMEM((8 * rows_tab, LANES), f32),
            pltpu.VMEM((4, UNROLL * SUB, LANES), f32),
            pltpu.VMEM((depth, 4 * cols), f32),
            pltpu.VMEM((n, 2, here, depth), f32),
            pltpu.VMEM((n, 2, here, 2 * cols), f32),
            pltpu.SemaphoreType.DMA((n,)),
            pltpu.SemaphoreType.DMA((n,)),
            pltpu.SemaphoreType.DMA((n,)),
            pltpu.SemaphoreType.DMA((n,)),
            pltpu.SemaphoreType.DMA,
        ],
        compiler_params=pltpu.CompilerParams(
            collective_id=0, has_side_effects=True, vmem_limit_bytes=40 * 1024 * 1024
        ),
    )(p_panel, eps_coef, inv_coef, wave, harmonics, harmonics, panel, row_target.reshape(1, -1))


def solution(mesh):
    in_specs = (
        P(None, ("freq", "row"), None),
        P("freq", None, None),
        P("freq", None, None),
        P("freq"),
        P(),
        P(),
        P(),
    )
    return jax.shard_map(
        functools.partial(on_device, mesh.shape["row"]),
        mesh=mesh,
        in_specs=in_specs,
        out_specs=P(None, ("freq", "row"), None),
        check_vma=False,
    )
```
